256 devices in a mesh: dp: 4 (over y), expert: 64 (over x, z, core).
Axes of the slice: x: 4, y: 4, z: 8, core: 2. Of those that a mesh axis runs over, the one named last changes fastest.
Arguments:
- tokens: bfloat16 [16384, 2048], P(('dp', 'expert')), may hold values from -6 to 6
- cotangent: bfloat16 [16384, 2048], P(('dp', 'expert')), may hold values from -6 to 6
- expert_ids: int32 [16384, 8], P(('dp', 'expert')), may hold values from 0 to 63, all different within a row; in each aligned block of 64 rows (0 to 63, 64 to 127, ...) at most 8 rows name the same one
- combine: float32 [16384, 8], P(('dp', 'expert')), may hold values from 0.05 to 0.6
- slot_table: int32 [64], replicated, may hold values from 0 to 63, each once
- swap_flags: int32 [32], replicated, may hold values 0 or 1
- weights: bfloat16 [64, 2048, 1152], P('expert', 'dp'), may hold values from -0.125 to 0.125
- moments: float32 [2, 64, 2048, 1152], P(None, 'expert', 'dp'), may hold values from -4.5254834 to 102.4, as said below
Outputs:
- layer_out: bfloat16 [16384, 2048], P(('dp', 'expert'))
- token_grad: bfloat16 [16384, 2048], P(('dp', 'expert'))
- update: bfloat16 [64, 2048, 1152], P('expert', 'dp')
The draws below stay inside these ranges and needn't reach their ends.
Inputs may be any that keep to these rules, and one draw needn't show every extreme that they name: `expert_ids`: in the rows of one device (aligned blocks of 64 tokens), no expert is named by more than 8 routes, a bound that some block reaches; a token's 8 experts differ. `slot_table`: A permutation: each slot holds one expert. moments[1] is positive.
All inputs are finite; a program needn't handle non-finite values.
Results may differ from the reference program's by a relative error of at most 0.0064.
Values may be sent and summed in bfloat16 or wider, within the bound.
A program may use at most 128 MiB of HBM per device.

```python
import math
import jax
import jax.numpy as jnp
import numpy as np
from jax import lax

D = 2048
FF = 384
TOP = 8
TOK_DEV = 64
EXPERTS = 64
TOKENS = 16384
CAP = 8
EXP_ROWS = 2048
N_DP = 4
N_EXPERT = 64


def draw_moments(key, part):
    key_first, key_second = jax.random.split(jax.random.fold_in(key, 17))
    shape = (EXPERTS, D, 3 * FF)
    spread = 0.05 * EXP_ROWS ** 0.5
    low_log = math.log(0.002 * EXP_ROWS)
    high_log = math.log(0.05 * EXP_ROWS)
    first_part = jnp.clip(jax.random.normal(key_first, shape, jnp.float32), -2.0, 2.0) * spread
    second_part = jnp.exp(jax.random.uniform(key_second, shape, jnp.float32, low_log, high_log))
    return jnp.stack([first_part, second_part])


def set_ends(values, own_key, least, largest):
    longest = values.shape.index(max(values.shape))
    spots = []
    for shift in (0, 1):
        where = [jax.random.randint(jax.random.fold_in(own_key, axis), (), 0, length) for axis, length in enumerate(values.shape)]
        where[longest] = (where[longest] + shift) % values.shape[longest]
        spots.append(tuple(where))
    return values.at[spots[0]].set(least).at[spots[1]].set(largest)


def level_of(key, dims, cuts, smallest, largest):
    def one(axis_at, parts):
        draws = jax.random.uniform(jax.random.fold_in(jax.random.fold_in(key, 6), axis_at), (parts,), jnp.float32, smallest / len(cuts), largest / len(cuts))
        return jnp.repeat(jnp.exp(draws), dims[axis_at] // parts).reshape((-1,) + (1,) * (len(dims) - axis_at - 1))

    factor_of = one(*cuts[0])
    for cut in cuts[1:]:
        factor_of = factor_of * one(*cut)
    return factor_of


def shared_out(rng, own, number, rows, number_of, top, bound, skew):
    sequence = jax.random.permutation(rng, number_of)
    heavy_load, usual = portions_of(number_of, rows * top, bound, skew, True), portions_of(number_of, rows * top, bound, skew, False)
    places = jnp.arange(number_of)

    def named(tallies, rotation):
        used = int((tallies > 0).sum())
        fixed = max(1, used // 4)
        shifted = fixed + (places - fixed + rotation * (used - fixed)) % max(1, number_of - fixed)
        return jnp.zeros((number_of,), jnp.int32).at[sequence[jnp.where(places < fixed, places, shifted)]].set(jnp.asarray(tallies, jnp.int32))

    tallies = jnp.where(number % 4 == 0, named(heavy_load, number // 4), named(usual, number - number // 4 - 1))
    mixed = jax.random.permutation(jax.random.fold_in(own, 3), number_of)
    source_of, receiver = mixed[0:number_of // 2 * 2:2], mixed[1:number_of // 2 * 2:2]
    margin = jnp.minimum(tallies[source_of] - 1, bound - tallies[receiver]) // 2
    margin = jnp.where((source_of == sequence[0]) | (receiver == sequence[0]) | (tallies[receiver] == 0), 0, jnp.maximum(margin, 0))
    shifted = jax.random.randint(jax.random.fold_in(own, 4), (number_of // 2,), 0, 1 << 20) % (margin + 1)
    tallies = tallies.at[source_of].add(-shifted).at[receiver].add(shifted)
    members = jnp.searchsorted(jnp.cumsum(tallies), jnp.arange(rows * top), side="right").astype(jnp.int32)
    table = members.reshape(top, rows).T
    table = table[jax.random.permutation(jax.random.fold_in(own, 1), rows)]
    rotation = jax.random.randint(jax.random.fold_in(own, 2), (rows, 1), 0, top)
    return jnp.take_along_axis(table, (jnp.arange(top)[None, :] + rotation) % top, axis=1)


def portions_of(count, total, limit, lean, full):
    portions = [(1 << 20) // math.isqrt(rank ** lean) + 1 for rank in range(1, count + 1)]
    largest = limit if full else min(limit, max(-(-total // count), total * portions[0] // sum(portions)))
    least = 1 if total - largest >= count - 1 else 0
    holding, spare = [largest] + [least] * (count - 1), total - largest - least * (count - 1)
    while spare > 0:
        movable = [i for i in range(1, count) if holding[i] < largest] or [i for i in range(1, count) if holding[i] < limit]
        pool, budget = sum([portions[i] for i in movable]), spare
        for i in movable:
            extra = min(limit - holding[i], max(1, budget * portions[i] // pool), spare)
            holding[i] = holding[i] + extra
            spare = spare - extra
    return np.array(holding)


def noise(rng, dims, scale, limit, pieces=(), kind=jnp.bfloat16):
    loudness = level_of(rng, dims, pieces, -0.22, 0.18) if pieces else 1.0
    values = jax.random.normal(rng, dims, jnp.float32) * scale * loudness
    return jnp.minimum(jnp.maximum(values, -limit), limit).astype(kind)


def setup_inputs(seed: int = 0) -> dict:
    seeds = jax.random.split(jax.random.key(seed), 9)
    tokens = noise(seeds[0], (TOKENS, D), 1.0, 6.0, ((0, 256),))
    cotangent = noise(seeds[1], (TOKENS, D), 1.0, 6.0, ((0, 256),))
    expert_ids_keys = jax.random.split(jax.random.fold_in(seeds[2], 1), TOKENS // TOK_DEV)
    expert_ids_turns = jax.random.permutation(jax.random.fold_in(seeds[2], 3), TOKENS // TOK_DEV)
    expert_ids = jax.vmap(lambda own, number: shared_out(jax.random.fold_in(seeds[2], 2), own, number, TOK_DEV, EXPERTS, TOP, CAP, 2))(expert_ids_keys, expert_ids_turns).reshape((TOKENS, TOP))
    combine = jnp.clip(jnp.exp(math.log(0.6) - 2.4849067 * jax.random.uniform(seeds[3], (TOKENS, TOP), jnp.float32) ** level_of(seeds[3], (TOKENS, TOP), ((0, 256),), -0.2, 0.2)), 0.05, 0.6)
    slot_table = jax.random.permutation(seeds[4], EXPERTS).astype(jnp.int32)
    swap_flags = set_ends((jax.random.randint(seeds[5], (EXPERTS // 2,), 0, 2) < 1).astype(jnp.int32), jax.random.fold_in(seeds[5], 1), 0, 1)
    weights = noise(seeds[6], (EXPERTS, D, 3 * FF), D ** -0.5, 0.125, ((0, 64), (1, 4)))
    moments = draw_moments(jax.random.fold_in(seeds[8], 71), 0)
    return dict(tokens=tokens, cotangent=cotangent, expert_ids=expert_ids, combine=combine, slot_table=slot_table, swap_flags=swap_flags, weights=weights, moments=moments)


beta_one = 0.9
beta_two = 0.999
adam_eps = 1e-08

def silu_parts(gate_pre):
    sigmoid = jax.nn.sigmoid(gate_pre)
    return (gate_pre * sigmoid, sigmoid * (1.0 + gate_pre * (1.0 - sigmoid)))

def reference(tokens, cotangent, expert_ids, combine, slot_table, swap_flags, weights, moments):
    routes = TOKENS * TOP
    slot_limit = N_DP * N_EXPERT * CAP
    half_count = EXPERTS // 2
    route_slot = slot_table[expert_ids.reshape(routes)]
    route_weight = combine.reshape(routes)
    route_index = jnp.arange(routes, dtype=jnp.int32)

    def per_slot(carry, slot_now):
        out_acc, grad_acc = carry
        is_here = route_slot == slot_now
        route_rank = jnp.cumsum(is_here.astype(jnp.int32)) - 1
        target = jnp.where(is_here, route_rank, slot_limit).astype(jnp.int32)
        owner_route = jnp.full((slot_limit,), routes, jnp.int32).at[target].set(route_index, mode='drop')
        filled = owner_route < routes
        route_pos = jnp.minimum(owner_route, routes - 1)
        token_of = route_pos // TOP
        route_scale = jnp.where(filled, route_weight[route_pos], jnp.zeros((), route_weight.dtype))
        expert_rows = jnp.where(filled[:, None], tokens[token_of], jnp.zeros((), tokens.dtype))
        grad_rows = (cotangent[token_of].astype(jnp.float32) * route_scale[:, None]).astype(jnp.bfloat16)
        gathered = lax.dynamic_index_in_dim(weights, slot_now, 0, keepdims=False)
        weight_in = gathered[:, :2 * FF]
        weight_out = gathered[:, 2 * FF:]
        projected = jnp.dot(expert_rows, weight_in, preferred_element_type=jnp.float32)
        gate_pre = projected[:, :FF]
        up_pre = projected[:, FF:]
        activated, silu_slope = silu_parts(gate_pre)
        hidden = (activated * up_pre).astype(jnp.bfloat16)
        out_rows = lax.dot_general(hidden, weight_out, (((1,), (1,)), ((), ())), preferred_element_type=jnp.float32).astype(jnp.bfloat16)
        d_hidden = jnp.dot(grad_rows, weight_out, preferred_element_type=jnp.float32)
        d_pre = jnp.concatenate([d_hidden * up_pre * silu_slope, d_hidden * activated], axis=1).astype(jnp.bfloat16)
        dx_rows = lax.dot_general(d_pre, weight_in, (((1,), (1,)), ((), ())), preferred_element_type=jnp.float32).astype(jnp.bfloat16)
        grad_in = lax.dot_general(expert_rows, d_pre, (((0,), (0,)), ((), ())), preferred_element_type=jnp.float32)
        grad_out = lax.dot_general(grad_rows, hidden, (((0,), (0,)), ((), ())), preferred_element_type=jnp.float32)
        weight_grad = jnp.concatenate([grad_in, grad_out], axis=1)
        moment_pair = lax.dynamic_index_in_dim(moments, slot_now, 1, keepdims=False)
        first_new = beta_one * moment_pair[0] + (1.0 - beta_one) * weight_grad
        second_new = beta_two * moment_pair[1] + (1.0 - beta_two) * weight_grad * weight_grad
        adam_step = (first_new / (jnp.sqrt(second_new) + adam_eps)).astype(jnp.bfloat16)
        out_acc = out_acc.at[token_of].add(route_scale[:, None] * out_rows.astype(jnp.float32))
        grad_acc = grad_acc.at[token_of].add(dx_rows.astype(jnp.float32))
        return ((out_acc, grad_acc), adam_step)
    empty_acc = jnp.zeros((TOKENS, D), jnp.float32)
    carried, all_steps = lax.scan(per_slot, (empty_acc, empty_acc), jnp.arange(EXPERTS, dtype=jnp.int32))
    out_acc, grad_acc = carried
    slot_range = jnp.arange(EXPERTS, dtype=jnp.int32)
    swapped_pair = swap_flags[slot_range % half_count] == 1
    source = jnp.where(swapped_pair, (slot_range + half_count) % EXPERTS, slot_range)
    update = all_steps[source]
    return (out_acc.astype(jnp.bfloat16), grad_acc.astype(jnp.bfloat16), update)
```

```python
import functools

import jax
import jax.numpy as jnp
from jax import lax
from jax.experimental import pallas as pl
from jax.experimental.pallas import tpu as pltpu
from jax.sharding import PartitionSpec as P

beta_one = 0.9
beta_two = 0.999
adam_eps = 1e-08
MESH = pl.DeviceIdType.MESH
bf16 = jnp.bfloat16
f32 = jnp.float32

NY, NX, NZ, NC = 4, 4, 8, 2
TOK = 64
D = 2048
HALF = D // 2
ROWS = 512
FF = 384
FF2 = 2 * FF
FF3 = 3 * FF
PART = D // NY
PIECE = PART // 4


def dot(a, b, ca=1, cb=0):
    return lax.dot_general(a, b, (((ca,), (cb,)), ((), ())), preferred_element_type=f32)


def kernel(
    flags, info_ref, tok_ref, cot_ref, w_ref, mom_ref,
    lo_ref, tg_ref, up_ref,
    info_all, pick, back_one, back_hi, back_lo, scale,
    near, xs, xr, wg, orow, orecv, rs_out, rs_in,
    gsend, gown, grecv, mom, uown, urecv, proj, hidden, d_pre,
    local_sem, info_sem, zsend, zrecv, xsend, xrecv, xlocal, wsend, wrecv,
    osend, orecv_sem, olocal, rsend, rrecv, gsend_sem, grecv_sem, usend, urecv_sem,
):
    y = lax.axis_index("dp")
    e = lax.axis_index("expert")
    x = lax.div(e, NZ * NC)
    z = lax.div(lax.rem(e, NZ * NC), NC)
    c = lax.rem(e, NC)
    me = x * NC + c

    def xdev(j):
        return (y, lax.div(j, NC) * (NZ * NC) + z * NC + lax.rem(j, NC))

    def zdev(k):
        return (y, x * (NZ * NC) + k * NC + c)

    def zat(off):
        return lax.rem(z + (off % NZ), NZ)

    def yat(off):
        return lax.rem(y + (off % NY), NY)

    znext = (zdev(zat(1)), zdev(zat(-1)))
    ynext = ((yat(1), e), (yat(-1), e))

    def rcopy(src, dst, ssem, rsem, dev):
        return pltpu.make_async_remote_copy(
            src_ref=src, dst_ref=dst, send_sem=ssem, recv_sem=rsem, device_id=dev, device_id_type=MESH
        )

    def await_bytes(ref, sem):
        pltpu.make_async_copy(ref, ref, sem).wait()

    mom_copy = pltpu.make_async_copy(mom_ref, mom, local_sem.at[0])
    mom_copy.start()
    w_copy = pltpu.make_async_copy(w_ref, wg.at[pl.ds(y * PART, PART)], local_sem.at[1])
    w_copy.start()

    bar = pltpu.get_barrier_semaphore()
    for r in range(1, 8):
        for dev in (xdev(lax.rem(me + r, 8)), zdev(zat(r))):
            pl.semaphore_signal(bar, inc=1, device_id=dev, device_id_type=MESH)
    for dev in ynext:
        pl.semaphore_signal(bar, inc=1, device_id=dev, device_id_type=MESH)
    pl.semaphore_wait(bar, 16)

    for r in range(1, NZ):
        rcopy(info_ref, info_all.at[z], info_sem.at[0], info_sem.at[1], zdev(zat(r))).start()

    def send_own(t):
        src = (tok_ref, cot_ref)[t]
        for h in (0, 1):
            for way in (0, 1):
                rcopy(
                    src.at[:, pl.ds(h * HALF, HALF)], near.at[t, z, h],
                    zsend.at[t, way], zrecv.at[t, way, 0, h], znext[way],
                ).start()

    send_own(0)
    for way in (0, 1):
        for h in (way, 1 - way):
            rows = pl.ds(h * (PART // 2), PART // 2)
            rcopy(
                w_ref.at[rows], wg.at[pl.ds(y * PART + h * (PART // 2), PART // 2)],
                wsend.at[way], wrecv.at[way, h], ynext[way],
            ).start()

    def weights_on():
        for way in (0, 1):
            base = yat(-1 if way == 0 else 1) * PART + way * (PART // 2)
            rows = wg.at[pl.ds(base, PART // 2)]
            await_bytes(rows, wrecv.at[way, way])
            rcopy(rows, rows, wsend.at[way], wrecv.at[way, 2], ynext[way]).start()

    def weights_in():
        w_copy.wait()
        for way in (0, 1):
            base = yat(-1 if way == 0 else 1) * PART + (1 - way) * (PART // 2)
            await_bytes(wg.at[pl.ds(base, PART // 2)], wrecv.at[way, 1 - way])
            base = yat(2) * PART + way * (PART // 2)
            await_bytes(wg.at[pl.ds(base, PART // 2)], wrecv.at[way, 2])

    info_all[z] = info_ref[...]
    await_bytes(info_all.at[pl.ds(0, NZ - 1)], info_sem.at[1])
    before = (
        lax.broadcasted_iota(jnp.int32, (128, 128), 0) < lax.broadcasted_iota(jnp.int32, (128, 128), 1)
    ).astype(f32)
    j_col = lax.broadcasted_iota(jnp.int32, (8, 128), 0)
    slots = ((j_col // NC) * (NZ * NC) + z * NC + j_col % NC).astype(f32)
    place = lax.broadcasted_iota(jnp.int32, (16, 128), 0)

    def tables(off, carry):
        one = info_all[lax.rem(z + off, NZ)]
        here = jnp.zeros((8, 128), f32)
        weight = jnp.zeros((8, 128), f32)
        for k in range(8):
            same = jnp.broadcast_to(one[k : k + 1], (8, 128)) == slots
            here = here + jnp.where(same, 1.0, 0.0)
            weight = weight + jnp.where(same, jnp.broadcast_to(one[8 + k : 9 + k], (8, 128)), 0.0)
        rank = dot(here, before)
        second = jnp.where((off >= 1) & (off <= 4), 1, 0)
        rank = jnp.where(here > 0.5, rank, 99.0)
        wanted = (place - second * 8).astype(f32)
        wanted = jnp.where((wanted >= 0.0) & (wanted < 8.0), wanted, -1.0)
        hot = []
        heavy = []
        for j in range(8):
            is_it = jnp.broadcast_to(rank[j : j + 1], (16, 128)) == wanted
            hot.append(jnp.where(is_it, 1.0, 0.0))
            heavy.append(jnp.where(is_it, jnp.broadcast_to(weight[j : j + 1], (16, 128)), 0.0))
        hot = jnp.concatenate(hot, axis=0)
        heavy = jnp.concatenate(heavy, axis=0)
        pick[off] = hot.astype(bf16)
        scale[off] = jnp.broadcast_to(jnp.sum(heavy, axis=1, keepdims=True), (128, 128))
        back_one[off] = hot.T.astype(bf16)
        turned = heavy.T
        high = turned.astype(bf16)
        back_hi[off] = high
        back_lo[off] = (turned - high.astype(f32)).astype(bf16)
        return carry

    lax.fori_loop(0, NZ, tables, 0)

    def gather(t, s, h, off_a, off_b, rows_a, rows_b):
        cols = pl.ds(h * HALF, HALF)
        rows = dot(pick[off_a][:, :TOK], rows_a) + dot(pick[off_b][:, :TOK], rows_b)
        if t == 1:
            rows = rows * (scale[off_a][:, :1] + scale[off_b][:, :1])
        xs[t, s, :, cols] = rows.astype(bf16)
        mine = pl.ds(me * 64 + s * 16, 16)

        def send(r, carry):
            j = lax.rem(me + r, 8)
            rcopy(
                xs.at[t, s, pl.ds(j * 16, 16), cols], xr.at[t, mine, cols],
                xsend.at[t], xrecv.at[t], xdev(j),
            ).start()
            return carry

        lax.fori_loop(1, 8, send, 0)
        pltpu.make_async_copy(xs.at[t, s, pl.ds(me * 16, 16), cols], xr.at[t, mine, cols], xlocal.at[t]).start()

    def step(t, s, h):
        for way in (0, 1):
            chunk = near.at[t, zat(-s if way == 0 else s), h]
            await_bytes(chunk, zrecv.at[t, way, s - 1, h])
            if s < 3 or h == way:
                rcopy(chunk, chunk, zsend.at[t, way], zrecv.at[t, way, s, h], znext[way]).start()
        gather(t, s, h, NZ - s, s, near[t, zat(-s), h], near[t, zat(s), h])

    def last_step(t, h):
        far = zat(4)
        await_bytes(near.at[t, far, h], zrecv.at[t, h, 3, h])
        own = (tok_ref, cot_ref)[t][:, h * HALF : (h + 1) * HALF]
        gather(t, 0, h, 0, 4, own, near[t, far, h])

    for s in (1, 2, 3):
        for h in (0, 1):
            step(0, s, h)
        if s == 2:
            send_own(1)
        if s == 3:
            weights_on()
    for h in (0, 1):
        last_step(0, h)
    for s in (1, 2, 3):
        for h in (0, 1):
            step(1, s, h)
    for h in (0, 1):
        last_step(1, h)

    def rows_in(t):
        await_bytes(xr.at[t, pl.ds(0, 448)], xrecv.at[t])
        await_bytes(xr.at[t, pl.ds(0, 64)], xlocal.at[t])

    rows_in(0)
    weights_in()

    def project(n, carry):
        cols = pl.ds(pl.multiple_of(n * 256, 256), 256)
        proj[:, cols] = dot(xr[0], wg[:, cols])
        return carry

    lax.fori_loop(0, 3, project, 0)

    def activate(n, carry):
        rows = pl.ds(pl.multiple_of(n * 64, 64), 64)
        gate = proj[rows, :FF]
        hidden[rows] = (gate * jax.nn.sigmoid(gate) * proj[rows, FF:]).astype(bf16)
        return carry

    lax.fori_loop(0, 8, activate, 0)

    def out_rows(n, carry):
        part = pl.ds(pl.multiple_of(n * 256, 256), 256)
        orow[0, :, part] = dot(hidden[...], wg[part, FF2:], 1, 1).astype(bf16)
        return carry

    lax.fori_loop(0, 8, out_rows, 0)

    def send_back(t):
        for s in (0, 3, 2, 1):
            def send(r, carry, s=s):
                j = lax.rem(me + r, 8)
                rcopy(
                    orow.at[t, pl.ds(j * 64 + s * 16, 16)], orecv.at[t, s, pl.ds(me * 16, 16)],
                    osend.at[t], orecv_sem.at[t, s], xdev(j),
                ).start()
                return carry

            lax.fori_loop(1, 8, send, 0)
            pltpu.make_async_copy(
                orow.at[t, pl.ds(me * 64 + s * 16, 16)], orecv.at[t, s, pl.ds(me * 16, 16)], olocal.at[t, s]
            ).start()

    send_back(0)

    rows_in(1)

    def backward(n, carry):
        rows = pl.ds(pl.multiple_of(n * 256, 256), 256)
        d_hidden = dot(xr[1, rows], wg[:, FF2:])
        gate = proj[rows, :FF]
        up = proj[rows, FF:]
        sig = jax.nn.sigmoid(gate)
        d_pre[rows, :FF] = (d_hidden * up * (sig * (1.0 + gate * (1.0 - sig)))).astype(bf16)
        d_pre[rows, FF:] = (d_hidden * (gate * sig)).astype(bf16)
        return carry

    lax.fori_loop(0, 2, backward, 0)

    def weight_grad(off, dest):
        base = yat(off) * PART

        def half(n, carry):
            cols = pl.ds(pl.multiple_of(base + n * 256, 256), 256)
            rows = pl.ds(pl.multiple_of(n * 256, 256), 256)
            dest[rows, :FF2] = dot(xr[0, :, cols], d_pre[...], 0, 0).astype(dest.dtype)
            dest[rows, FF2:] = dot(xr[1, :, cols], hidden[...], 0, 0).astype(dest.dtype)
            return carry

        lax.fori_loop(0, 2, half, 0)

    def send_grad(way, message, block, piece):
        rcopy(
            gsend.at[block, pl.ds(piece * PIECE, PIECE)], grecv.at[way, message],
            gsend_sem.at[way], grecv_sem.at[way, message], ynext[way],
        ).start()

    weight_grad(2, gsend.at[0])
    send_grad(0, 0, 0, 0)
    send_grad(1, 0, 0, 2)
    weight_grad(1, gsend.at[1])
    send_grad(0, 1, 1, 2)
    weight_grad(-1, gsend.at[2])
    send_grad(1, 1, 2, 0)

    def pass_on(first):
        for way in (0, 1):
            message = 0 if first else 3
            piece = (0 if way == 0 else 2) + (0 if first else 1)
            await_bytes(grecv.at[way, message], grecv_sem.at[way, message])

            def add(n, carry, way=way, message=message, piece=piece):
                there = pl.ds(pl.multiple_of(piece * PIECE + n * 16, 16), 16)
                here = pl.ds(pl.multiple_of(n * 16, 16), 16)
                total = gsend[1 + way, there].astype(f32) + grecv[way, message, here].astype(f32)
                gsend[1 + way, there] = total.astype(bf16)
                return carry

            lax.fori_loop(0, PIECE // 16, add, 0)
            send_grad(way, message + 2, 1 + way, piece)

    def second_round():
        send_grad(0, 3, 0, 1)
        send_grad(1, 3, 0, 3)
        send_grad(0, 4, 1, 3)
        send_grad(1, 4, 2, 1)

    def adam(first):
        for low in (True, False):
            piece = (0 if low else 2) + (0 if first else 1)
            done, plain = (2, 1) if first else (5, 4)
            from_low, from_high = (done, plain) if low else (plain, done)
            await_bytes(grecv.at[0, from_low], grecv_sem.at[0, from_low])
            await_bytes(grecv.at[1, from_high], grecv_sem.at[1, from_high])

            def rows_of(n, carry, piece=piece, from_low=from_low, from_high=from_high):
                there = pl.ds(pl.multiple_of(piece * PIECE + n * 16, 16), 16)
                here = pl.ds(pl.multiple_of(n * 16, 16), 16)
                grad = gown[there] + grecv[0, from_low, here].astype(f32) + grecv[1, from_high, here].astype(f32)
                first_new = beta_one * mom[0, there] + (1.0 - beta_one) * grad
                second_new = beta_two * mom[1, there] + (1.0 - beta_two) * grad * grad
                uown[there] = (first_new / (jnp.sqrt(second_new) + adam_eps)).astype(bf16)
                return carry

            lax.fori_loop(0, PIECE // 16, rows_of, 0)
            rows = pl.ds(piece * PIECE, PIECE)
            rcopy(
                uown.at[rows], urecv.at[rows], usend.at[0], urecv_sem.at[piece],
                xdev(lax.rem(me + 4, 8)),
            ).start()

    def partial(t, off, s, cols):
        rows = orecv[t, s, :, cols]
        if t == 1:
            return dot(back_one[off][:TOK], rows)
        return dot(back_hi[off][:TOK], rows) + dot(back_lo[off][:TOK], rows)

    def over_tiles(h, body):
        def tile(n, carry):
            inner = pl.multiple_of(n * 256, 256)
            body(pl.ds(pl.multiple_of(h * HALF + inner, 256), 256), pl.ds(inner, 256))
            return carry

        lax.fori_loop(0, HALF // 256, tile, 0)

    def reduce_step(t, k):
        s = (4 - k) % 4
        await_bytes(orecv.at[t, s, pl.ds(0, 112)], orecv_sem.at[t, s])
        await_bytes(orecv.at[t, s, pl.ds(0, 16)], olocal.at[t, s])
        for way in (0, 1):
            off = (4 - k) if way == 0 else (4 + k)
            if k == 1:
                await_bytes(rs_in.at[t, way, 0, way], rrecv.at[t, way, 0])
            if k > 1:
                await_bytes(rs_in.at[t, way, k - 1], rrecv.at[t, way, k - 1])
            for h in (0, 1):
                if k == 0 and h != way:
                    continue

                def one(cols, inner, way=way, off=off, h=h):
                    total = partial(t, off, s, cols)
                    if k > 1 or (k == 1 and h == way):
                        total = total + rs_in[t, way, k - 1, h, :, inner].astype(f32)
                    rs_out[t, way, k, h, :, inner] = total.astype(bf16)

                over_tiles(h, one)
            out, into = rs_out.at[t, way, k], rs_in.at[t, way, k]
            if k == 0:
                out, into = out.at[way], into.at[way]
            rcopy(out, into, rsend.at[t, way, k], rrecv.at[t, way, k], znext[way]).start()

    def reduce_last(t):
        for way in (0, 1):
            await_bytes(rs_in.at[t, way, 3], rrecv.at[t, way, 3])
        for h in (0, 1):
            def one(cols, inner, h=h):
                total = partial(t, 0, 0, cols)
                total = total + rs_in[t, 0, 3, h, :, inner].astype(f32) + rs_in[t, 1, 3, h, :, inner].astype(f32)
                (lo_ref, tg_ref)[t][:, cols] = total.astype(bf16)

            over_tiles(h, one)

    reduce_step(0, 0)

    def dx_rows(n, carry):
        part = pl.ds(pl.multiple_of(n * 256, 256), 256)
        orow[1, :, part] = dot(d_pre[...], wg[part, :FF2], 1, 1).astype(bf16)
        return carry

    lax.fori_loop(0, 8, dx_rows, 0)
    send_back(1)
    pass_on(True)
    second_round()
    reduce_step(0, 1)
    weight_grad(0, gown)
    mom_copy.wait()
    reduce_step(0, 2)
    reduce_step(0, 3)
    adam(True)
    reduce_step(1, 0)
    reduce_last(0)
    pass_on(False)
    reduce_step(1, 1)
    reduce_step(1, 2)
    adam(False)
    reduce_step(1, 3)
    reduce_last(1)

    swapped = jnp.full((16, FF3), flags[lax.rem(e, NX * NZ * NC // 2)], jnp.int32) == 1
    for piece in (0, 2, 1, 3):
        await_bytes(urecv.at[pl.ds(piece * PIECE, PIECE)], urecv_sem.at[piece])

        def choose(n, carry, piece=piece):
            there = pl.ds(pl.multiple_of(piece * PIECE + n * 16, 16), 16)
            up_ref[there] = jnp.where(swapped, urecv[there].astype(f32), uown[there].astype(f32)).astype(bf16)
            return carry

        lax.fori_loop(0, PIECE // 16, choose, 0)

    await_bytes(info_all.at[pl.ds(0, NZ - 1)], info_sem.at[0])
    await_bytes(uown, usend.at[0])
    for way in (0, 1):
        await_bytes(wg.at[pl.ds(0, PART + PART // 2)], wsend.at[way])
        await_bytes(grecv.at[way], gsend_sem.at[way])
    for t in (0, 1):
        await_bytes(xr.at[t, pl.ds(0, 448)], xsend.at[t])
        await_bytes(orow.at[t, pl.ds(0, 448)], osend.at[t])
        for way in (0, 1):
            await_bytes(near.at[t, pl.ds(0, 7), 0], zsend.at[t, way])
            await_bytes(rs_out.at[t, way, 0, way], rsend.at[t, way, 0])
            for k in (1, 2, 3):
                await_bytes(rs_out.at[t, way, k], rsend.at[t, way, k])


def local(tokens, cotangent, expert_ids, combine, slot_table, swap_flags, weights, moments):
    experts = slot_table.shape[0]
    slot_range = jnp.arange(experts, dtype=jnp.int32)
    turned = expert_ids.T
    slots = jnp.sum(
        jnp.where(turned[:, :, None] == slot_range[None, None, :], slot_table[None, None, :], 0), axis=2
    )
    info = jnp.concatenate([slots.astype(f32), combine.T], axis=0)
    info = jnp.pad(info, ((0, 0), (0, 128 - TOK)), constant_values=-1.0)
    vmem = pl.BlockSpec(memory_space=pltpu.VMEM)
    anyw = pl.BlockSpec(memory_space=pl.ANY)
    dma = pltpu.SemaphoreType.DMA
    layer_out, token_grad, update = pl.pallas_call(
        kernel,
        out_shape=(
            jax.ShapeDtypeStruct((TOK, D), bf16),
            jax.ShapeDtypeStruct((TOK, D), bf16),
            jax.ShapeDtypeStruct((PART, FF3), bf16),
        ),
        in_specs=[pl.BlockSpec(memory_space=pltpu.SMEM), vmem, vmem, vmem, anyw, anyw],
        out_specs=(vmem, vmem, vmem),
        scratch_shapes=[
            pltpu.VMEM((NZ, 16, 128), f32),
            pltpu.VMEM((NZ, 128, 128), bf16),
            pltpu.VMEM((NZ, 128, 128), bf16),
            pltpu.VMEM((NZ, 128, 128), bf16),
            pltpu.VMEM((NZ, 128, 128), bf16),
            pltpu.VMEM((NZ, 128, 128), f32),
            pltpu.VMEM((2, NZ, 2, TOK, HALF), bf16),
            pltpu.VMEM((2, 4, 128, D), bf16),
            pltpu.VMEM((2, ROWS, D), bf16),
            pltpu.VMEM((D, FF3), bf16),
            pltpu.VMEM((2, ROWS, D), bf16),
            pltpu.VMEM((2, 4, 128, D), bf16),
            pltpu.VMEM((2, 2, 4, 2, TOK, HALF), bf16),
            pltpu.VMEM((2, 2, 4, 2, TOK, HALF), bf16),
            pltpu.VMEM((3, PART, FF3), bf16),
            pltpu.VMEM((PART, FF3), f32),
            pltpu.VMEM((2, 6, PIECE, FF3), bf16),
            pltpu.VMEM((2, PART, FF3), f32),
            pltpu.VMEM((PART, FF3), bf16),
            pltpu.VMEM((PART, FF3), bf16),
            pltpu.VMEM((ROWS, FF2), f32),
            pltpu.VMEM((ROWS, FF), bf16),
            pltpu.VMEM((ROWS, FF2), bf16),
            dma((2,)),
            dma((2,)),
            dma((2, 2)),
            dma((2, 2, 4, 2)),
            dma((2,)),
            dma((2,)),
            dma((2,)),
            dma((2,)),
            dma((2, 3)),
            dma((2,)),
            dma((2, 4)),
            dma((2, 4)),
            dma((2, 2, 4)),
            dma((2, 2, 4)),
            dma((2,)),
            dma((2, 6)),
            dma((1,)),
            dma((4,)),
        ],
        compiler_params=pltpu.CompilerParams(
            collective_id=0, has_side_effects=True, vmem_limit_bytes=62 * 2**20
        ),
        cost_estimate=pl.CostEstimate(flops=8 * 10**9, bytes_accessed=9 * 10**6, transcendentals=10**6),
        name="moe_step",
    )(swap_flags, info, tokens, cotangent, weights[0], moments[:, 0])
    return layer_out, token_grad, update[None]


def solution(mesh):
    in_specs = (
        P(("dp", "expert"), None),
        P(("dp", "expert"), None),
        P(("dp", "expert"), None),
        P(("dp", "expert"), None),
        P(),
        P(),
        P("expert", "dp", None),
        P(None, "expert", "dp", None),
    )
    out_specs = (P(("dp", "expert"), None), P(("dp", "expert"), None), P("expert", "dp", None))
    return jax.shard_map(local, mesh=mesh, in_specs=in_specs, out_specs=out_specs, check_vma=False)
```

```python
import functools

import jax
import jax.numpy as jnp
from jax import lax
from jax.experimental import pallas as pl
from jax.experimental.pallas import tpu as pltpu
from jax.sharding import PartitionSpec as P

beta_one = 0.9
beta_two = 0.999
adam_eps = 1e-08
MESH = pl.DeviceIdType.MESH
bf16 = jnp.bfloat16
f32 = jnp.float32

NY, NX, NZ, NC = 4, 4, 8, 2
TOK = 64
D = 2048
HALF = D // 2
ROWS = 512
FF = 384
FF2 = 2 * FF
FF3 = 3 * FF
PART = D // NY
PIECE = PART // 4


def dot(a, b, ca=1, cb=0):
    return lax.dot_general(a, b, (((ca,), (cb,)), ((), ())), preferred_element_type=f32)


def kernel(
    flags, table, ids_ref, comb_ref, tok_ref, cot_ref, w_ref, mom_ref,
    lo_ref, tg_ref, up_ref,
    info_ref, info_all, sums, upd, fold, pick, xs_alone, back_one, back_hi, back_lo, scale,
    near, xs, xr, wg, orow, orecv, rs_out, rs_in,
    gsend, gown, grecv, mom, uown, urecv, proj, hidden, d_pre,
    local_sem, info_sem, zsend, zrecv, xsend, xrecv, xlocal, xsend_alone, frecv, flocal, out_sem, wsend, wrecv,
    osend, orecv_sem, olocal, rsend, rrecv, gsend_sem, grecv_sem, usend, urecv_sem,
):
    y = lax.axis_index("dp")
    e = lax.axis_index("expert")
    x = lax.div(e, NZ * NC)
    z = lax.div(lax.rem(e, NZ * NC), NC)
    c = lax.rem(e, NC)
    me = x * NC + c

    def xdev(j):
        return (y, lax.div(j, NC) * (NZ * NC) + z * NC + lax.rem(j, NC))

    def zdev(k):
        return (y, x * (NZ * NC) + k * NC + c)

    def zat(off):
        return lax.rem(z + (off % NZ), NZ)

    def yat(off):
        return lax.rem(y + (off % NY), NY)

    znext = (zdev(zat(1)), zdev(zat(-1)))
    ynext = ((yat(1), e), (yat(-1), e))

    def rcopy(src, dst, ssem, rsem, dev):
        return pltpu.make_async_remote_copy(
            src_ref=src, dst_ref=dst, send_sem=ssem, recv_sem=rsem, device_id=dev, device_id_type=MESH
        )

    def await_bytes(ref, sem):
        pltpu.make_async_copy(ref, ref, sem).wait()

    mom_copy = pltpu.make_async_copy(mom_ref, mom, local_sem.at[0])
    mom_copy.start()
    w_copy = pltpu.make_async_copy(w_ref, wg.at[pl.ds(y * PART, PART)], local_sem.at[1])
    w_copy.start()

    ids = ids_ref[...]

    def look_up(n, slot):
        return jnp.where(ids == n, table[n], slot)

    slot_of = lax.fori_loop(0, NX * NZ * NC, look_up, jnp.zeros((8, TOK), jnp.int32), unroll=4)
    info_ref[...] = jnp.full((16, 128), -1.0, f32)
    info_ref[0:8, :TOK] = slot_of.astype(f32)
    info_ref[8:16, :TOK] = comb_ref[...]

    bar = pltpu.get_barrier_semaphore()
    for r in range(1, 8):
        for dev in (xdev(lax.rem(me + r, 8)), zdev(zat(r))):
            pl.semaphore_signal(bar, inc=1, device_id=dev, device_id_type=MESH)
    for dev in ynext:
        pl.semaphore_signal(bar, inc=1, device_id=dev, device_id_type=MESH)
    pl.semaphore_wait(bar, 16)

    def send_own(t, h):
        src = (tok_ref, cot_ref)[t]
        for way in (0, 1):
            rcopy(
                src.at[:, pl.ds(h * HALF, HALF)], near.at[t, z, h],
                zsend.at[t, way], zrecv.at[t, way, 0, h], znext[way],
            ).start()

    send_own(0, 0)
    for r in range(1, NZ):
        rcopy(info_ref, info_all.at[z], info_sem.at[0], info_sem.at[1], zdev(zat(r))).start()
    for way in (0, 1):
        for h in (way, 1 - way):
            rows = pl.ds(h * (PART // 2), PART // 2)
            rcopy(
                w_ref.at[rows], wg.at[pl.ds(y * PART + h * (PART // 2), PART // 2)],
                wsend.at[way], wrecv.at[way, h], ynext[way],
            ).start()

    def weights_on():
        for way in (0, 1):
            base = yat(-1 if way == 0 else 1) * PART + way * (PART // 2)
            rows = wg.at[pl.ds(base, PART // 2)]
            await_bytes(rows, wrecv.at[way, way])
            rcopy(rows, rows, wsend.at[way], wrecv.at[way, 2], ynext[way]).start()

    def weights_in():
        w_copy.wait()
        for way in (0, 1):
            base = yat(-1 if way == 0 else 1) * PART + (1 - way) * (PART // 2)
            await_bytes(wg.at[pl.ds(base, PART // 2)], wrecv.at[way, 1 - way])
            base = yat(2) * PART + way * (PART // 2)
            await_bytes(wg.at[pl.ds(base, PART // 2)], wrecv.at[way, 2])

    info_all[z] = info_ref[...]
    before = (
        lax.broadcasted_iota(jnp.int32, (128, 128), 0) < lax.broadcasted_iota(jnp.int32, (128, 128), 1)
    ).astype(f32)
    j_col = lax.broadcasted_iota(jnp.int32, (8, 128), 0)
    slots = ((j_col // NC) * (NZ * NC) + z * NC + j_col % NC).astype(f32)
    place = lax.broadcasted_iota(jnp.int32, (16, 128), 0)

    def tables(off, carry):
        off = jnp.asarray(off, jnp.int32)
        one = info_all[lax.rem(z + off, NZ)]
        here = jnp.zeros((8, 128), f32)
        weight = jnp.zeros((8, 128), f32)
        for k in range(8):
            same = jnp.broadcast_to(one[k : k + 1], (8, 128)) == slots
            here = here + jnp.where(same, 1.0, 0.0)
            weight = weight + jnp.where(same, jnp.broadcast_to(one[8 + k : 9 + k], (8, 128)), 0.0)
        rank = dot(here, before)
        second = jnp.where((off >= 1) & (off <= 4), 1, 0)
        rank = jnp.where(here > 0.5, rank, 99.0)
        wanted = (place - second * 8).astype(f32)
        wanted = jnp.where((wanted >= 0.0) & (wanted < 8.0), wanted, -1.0)
        hot = []
        heavy = []
        for j in range(8):
            is_it = jnp.broadcast_to(rank[j : j + 1], (16, 128)) == wanted
            hot.append(jnp.where(is_it, 1.0, 0.0))
            heavy.append(jnp.where(is_it, jnp.broadcast_to(weight[j : j + 1], (16, 128)), 0.0))
        hot = jnp.concatenate(hot, axis=0)
        heavy = jnp.concatenate(heavy, axis=0)
        pick[off] = hot.astype(bf16)
        scale[off] = jnp.broadcast_to(jnp.sum(heavy, axis=1, keepdims=True), (128, 128))
        back_one[off] = hot.T.astype(bf16)
        turned = heavy.T
        high = turned.astype(bf16)
        back_hi[off] = high
        back_lo[off] = (turned - high.astype(f32)).astype(bf16)
        return carry

    tables(0, 0)
    def pack(t, off_a, rows_a, off_b, rows_b):
        rows = dot(pick[off_a][:, :TOK], rows_a) + dot(pick[off_b][:, :TOK], rows_b)
        if t == 1:
            weight = scale[off_a][:, :1]
            rows = rows * (weight if off_a == off_b else weight + scale[off_b][:, :1])
        return rows.astype(bf16)

    def spread(src, dst, there, sems):
        ssem, rsem, lsem = sems

        def send(r, carry):
            j = lax.rem(me + r, 8)
            rcopy(src(j), dst(there), ssem, rsem, xdev(j)).start()
            return carry

        lax.fori_loop(1, 8, send, 0)
        pltpu.make_async_copy(src(me), dst(there), lsem).start()

    def gather(t, s, h, off_a, off_b, rows_a, rows_b):
        cols = pl.ds(h * HALF, HALF)
        xs[t, s - 1, :, cols] = pack(t, off_a, rows_a, off_b, rows_b)
        spread(
            lambda j: xs.at[t, s - 1, pl.ds(j * 16, 16), cols], lambda at: xr.at[t, pl.ds(at, 16), cols],
            me * 64 + s * 16, (xsend.at[t], xrecv.at[t], xlocal.at[t]),
        )

    def gather_alone(t, which, off, low, high):
        cut = 120 if which == 0 else 8

        def turn(value):
            return jnp.concatenate([value[cut:], value[:cut]], axis=0)

        rows = dot(pick[off][:, :TOK], low) + dot(turn(pick[off])[:, :TOK], high)
        if t == 1:
            weight = scale[off]
            rows = rows * (weight + turn(weight))[:, :1]
        xs_alone[t, which] = rows.astype(bf16)
        spread(
            lambda j: xs_alone.at[t, which, pl.ds(j * 16, 16)], lambda at: fold.at[t, which, pl.ds(at, 16)],
            me * 16, (xsend_alone.at[t], frecv.at[t, which], flocal.at[t, which]),
        )

    def step(t, s, h):
        for way in (0, 1):
            chunk = near.at[t, zat(-s if way == 0 else s), h]
            await_bytes(chunk, zrecv.at[t, way, s - 1, h])
            if s < 3 or h == way:
                rcopy(chunk, chunk, zsend.at[t, way], zrecv.at[t, way, s, h], znext[way]).start()
        gather(t, s, h, NZ - s, s, near[t, zat(-s), h], near[t, zat(s), h])

    def own_step(t):
        src = (tok_ref, cot_ref)[t]
        gather_alone(t, 0, 0, src[:, :HALF], src[:, HALF:])

    def far_step(t):
        far = zat(4)
        for h in (0, 1):
            await_bytes(near.at[t, far, h], zrecv.at[t, h, 3, h])
        gather_alone(t, 1, 4, near[t, far, 0], near[t, far, 1])

    send_own(0, 1)
    own_step(0)
    own_step(1)
    await_bytes(info_all.at[pl.ds(0, NZ - 1)], info_sem.at[1])
    lax.fori_loop(1, NZ, tables, 0)
    step(0, 1, 0)
    step(0, 1, 1)
    send_own(1, 0)
    send_own(1, 1)
    step(0, 2, 0)
    step(0, 2, 1)
    step(1, 1, 0)
    step(1, 1, 1)
    weights_on()
    step(0, 3, 0)
    step(0, 3, 1)
    step(1, 2, 0)
    step(1, 2, 1)
    far_step(0)
    step(1, 3, 0)
    step(1, 3, 1)
    far_step(1)

    def rows_in(t):
        for which in (0, 1):
            await_bytes(fold.at[t, which, pl.ds(0, 112)], frecv.at[t, which])
            await_bytes(fold.at[t, which, pl.ds(0, 16)], flocal.at[t, which])

        def unfold(j, carry):
            block = pl.ds(pl.multiple_of(j * 16, 16), 16)
            own, far = fold[t, 0, block].astype(f32), fold[t, 1, block].astype(f32)
            into = pl.ds(pl.multiple_of(j * 64, 64), 16)
            xr[t, into, :HALF] = jnp.concatenate([own[:8], far[8:]], axis=0).astype(bf16)
            xr[t, into, HALF:] = jnp.concatenate([own[8:], far[:8]], axis=0).astype(bf16)
            return carry

        lax.fori_loop(0, 8, unfold, 0)
        await_bytes(xr.at[t, pl.ds(0, 336)], xrecv.at[t])
        await_bytes(xr.at[t, pl.ds(0, 48)], xlocal.at[t])

    rows_in(0)
    weights_in()

    def project(n, carry):
        cols = pl.ds(pl.multiple_of(n * 256, 256), 256)
        proj[:, cols] = dot(xr[0], wg[:, cols])
        return carry

    lax.fori_loop(0, 3, project, 0)

    def activate(n, carry):
        rows = pl.ds(pl.multiple_of(n * 64, 64), 64)
        gate = proj[rows, :FF]
        hidden[rows] = (gate * jax.nn.sigmoid(gate) * proj[rows, FF:]).astype(bf16)
        return carry

    lax.fori_loop(0, 8, activate, 0)

    def out_rows(n, carry):
        part = pl.ds(pl.multiple_of(n * 256, 256), 256)
        orow[0, :, part] = dot(hidden[...], wg[part, FF2:], 1, 1).astype(bf16)
        return carry

    lax.fori_loop(0, 8, out_rows, 0)

    def send_back(t, s):
        spread(
            lambda j: orow.at[t, pl.ds(j * 64 + s * 16, 16)], lambda at: orecv.at[t, s, pl.ds(at, 16)],
            me * 16, (osend.at[t], orecv_sem.at[t, s], olocal.at[t, s]),
        )

    send_back(0, 0)
    send_back(0, 3)

    rows_in(1)

    def backward(n, carry):
        rows = pl.ds(pl.multiple_of(n * 256, 256), 256)
        d_hidden = dot(xr[1, rows], wg[:, FF2:])
        gate = proj[rows, :FF]
        up = proj[rows, FF:]
        sig = jax.nn.sigmoid(gate)
        d_pre[rows, :FF] = (d_hidden * up * (sig * (1.0 + gate * (1.0 - sig)))).astype(bf16)
        d_pre[rows, FF:] = (d_hidden * (gate * sig)).astype(bf16)
        return carry

    lax.fori_loop(0, 2, backward, 0)

    def weight_grad(off, dest):
        base = yat(off) * PART

        def half(n, carry):
            cols = pl.ds(pl.multiple_of(base + n * 256, 256), 256)
            rows = pl.ds(pl.multiple_of(n * 256, 256), 256)
            dest[rows, :FF2] = dot(xr[0, :, cols], d_pre[...], 0, 0).astype(dest.dtype)
            dest[rows, FF2:] = dot(xr[1, :, cols], hidden[...], 0, 0).astype(dest.dtype)
            return carry

        lax.fori_loop(0, 2, half, 0)

    def send_grad(way, message, block, piece):
        rcopy(
            gsend.at[block, pl.ds(piece * PIECE, PIECE)], grecv.at[way, message],
            gsend_sem.at[way], grecv_sem.at[way, message], ynext[way],
        ).start()

    def pass_on(first):
        for way in (0, 1):
            message = 0 if first else 3
            piece = (0 if way == 0 else 2) + (0 if first else 1)
            await_bytes(grecv.at[way, message], grecv_sem.at[way, message])

            def add(n, carry, way=way, message=message, piece=piece):
                there = pl.ds(pl.multiple_of(piece * PIECE + n * 16, 16), 16)
                here = pl.ds(pl.multiple_of(n * 16, 16), 16)
                total = gsend[1 + way, there].astype(f32) + grecv[way, message, here].astype(f32)
                gsend[1 + way, there] = total.astype(bf16)
                return carry

            lax.fori_loop(0, PIECE // 16, add, 0)
            send_grad(way, message + 2, 1 + way, piece)

    def second_round():
        send_grad(0, 3, 0, 1)
        send_grad(1, 3, 0, 3)
        send_grad(0, 4, 1, 3)
        send_grad(1, 4, 2, 1)

    def adam(first):
        for low in (True, False):
            piece = (0 if low else 2) + (0 if first else 1)
            done, plain = (2, 1) if first else (5, 4)
            from_low, from_high = (done, plain) if low else (plain, done)
            await_bytes(grecv.at[0, from_low], grecv_sem.at[0, from_low])
            await_bytes(grecv.at[1, from_high], grecv_sem.at[1, from_high])

            def rows_of(n, carry, piece=piece, from_low=from_low, from_high=from_high):
                there = pl.ds(pl.multiple_of(piece * PIECE + n * 16, 16), 16)
                here = pl.ds(pl.multiple_of(n * 16, 16), 16)
                grad = gown[there] + grecv[0, from_low, here].astype(f32) + grecv[1, from_high, here].astype(f32)
                first_new = beta_one * mom[0, there] + (1.0 - beta_one) * grad
                second_new = beta_two * mom[1, there] + (1.0 - beta_two) * grad * grad
                uown[there] = (first_new / (jnp.sqrt(second_new) + adam_eps)).astype(bf16)
                return carry

            lax.fori_loop(0, PIECE // 16, rows_of, 0)
            rows = pl.ds(piece * PIECE, PIECE)
            rcopy(
                uown.at[rows], urecv.at[rows], usend.at[0], urecv_sem.at[piece],
                xdev(lax.rem(me + 4, 8)),
            ).start()

    def partial(t, off, s, cols):
        rows = orecv[t, s, :, cols]
        if t == 1:
            return dot(back_one[off][:TOK], rows)
        return dot(back_hi[off][:TOK], rows) + dot(back_lo[off][:TOK], rows)

    def over_tiles(h, body):
        def tile(n, carry):
            inner = pl.multiple_of(n * 256, 256)
            body(pl.ds(pl.multiple_of(h * HALF + inner, 256), 256), pl.ds(inner, 256))
            return carry

        lax.fori_loop(0, HALF // 256, tile, 0)

    def reduce_step(t, k):
        s = (4 - k) % 4
        await_bytes(orecv.at[t, s, pl.ds(0, 112)], orecv_sem.at[t, s])
        await_bytes(orecv.at[t, s, pl.ds(0, 16)], olocal.at[t, s])
        for turn in (0, 1):
            for way in (0, 1):
                off = (4 - k) if way == 0 else (4 + k)
                h = way if turn == 1 else 1 - way
                if k == 0 and h != way:
                    continue
                adds = k > 1 or (k == 1 and h == way)
                if adds:
                    await_bytes(rs_in.at[t, way, k - 1, h], rrecv.at[t, way, k - 1, h])

                def one(cols, inner):
                    total = partial(t, off, s, cols)
                    if adds:
                        total = total + rs_in[t, way, k - 1, h, :, inner].astype(f32)
                    rs_out[t, way, k, h, :, inner] = total.astype(bf16)

                over_tiles(h, one)
                rcopy(
                    rs_out.at[t, way, k, h], rs_in.at[t, way, k, h],
                    rsend.at[t, way], rrecv.at[t, way, k, h], znext[way],
                ).start()

    def reduce_last(t):
        for h in (0, 1):
            for way in (0, 1):
                await_bytes(rs_in.at[t, way, 3, h], rrecv.at[t, way, 3, h])

            def one(cols, inner):
                total = partial(t, 0, 0, cols)
                total = total + rs_in[t, 0, 3, h, :, inner].astype(f32) + rs_in[t, 1, 3, h, :, inner].astype(f32)
                sums[t, :, cols] = total.astype(bf16)

            over_tiles(h, one)
        pltpu.make_async_copy(sums.at[t], (lo_ref, tg_ref)[t], out_sem.at[t]).start()

    def dx_rows(n, carry):
        part = pl.ds(pl.multiple_of(n * 256, 256), 256)
        orow[1, :, part] = dot(d_pre[...], wg[part, :FF2], 1, 1).astype(bf16)
        return carry

    weight_grad(2, gsend.at[0])
    send_grad(0, 0, 0, 0)
    send_grad(1, 0, 0, 2)
    send_back(0, 2)
    weight_grad(1, gsend.at[1])
    weight_grad(-1, gsend.at[2])
    send_grad(0, 1, 1, 2)
    send_grad(1, 1, 2, 0)
    lax.fori_loop(0, 8, dx_rows, 0)
    send_back(0, 1)
    reduce_step(0, 0)
    send_back(1, 0)
    pass_on(True)
    reduce_step(0, 1)
    send_back(1, 3)
    weight_grad(0, gown)
    mom_copy.wait()
    second_round()
    reduce_step(0, 2)
    send_back(1, 2)
    reduce_step(0, 3)
    send_back(1, 1)
    adam(True)
    reduce_step(1, 0)
    pass_on(False)
    reduce_last(0)
    reduce_step(1, 1)
    reduce_step(1, 2)
    adam(False)
    reduce_step(1, 3)
    reduce_last(1)

    swapped = jnp.full((16, FF3), flags[lax.rem(e, NX * NZ * NC // 2)], jnp.int32) == 1
    for piece in (0, 2, 1, 3):
        await_bytes(urecv.at[pl.ds(piece * PIECE, PIECE)], urecv_sem.at[piece])

        def choose(n, carry, piece=piece):
            there = pl.ds(pl.multiple_of(piece * PIECE + n * 16, 16), 16)
            upd[there] = jnp.where(swapped, urecv[there].astype(f32), uown[there].astype(f32)).astype(bf16)
            return carry

        lax.fori_loop(0, PIECE // 16, choose, 0)
        rows = pl.ds(piece * PIECE, PIECE)
        pltpu.make_async_copy(upd.at[rows], up_ref.at[rows], out_sem.at[2]).start()

    for t in (0, 1):
        await_bytes(sums.at[t], out_sem.at[t])
    await_bytes(upd, out_sem.at[2])
    await_bytes(info_all.at[pl.ds(0, NZ - 1)], info_sem.at[0])
    await_bytes(uown, usend.at[0])
    for way in (0, 1):
        await_bytes(wg.at[pl.ds(0, PART + PART // 2)], wsend.at[way])
        await_bytes(grecv.at[way], gsend_sem.at[way])
    for t in (0, 1):
        await_bytes(xr.at[t, pl.ds(0, 336)], xsend.at[t])
        await_bytes(xs_alone.at[t, :, pl.ds(0, 112)], xsend_alone.at[t])
        await_bytes(orow.at[t, pl.ds(0, 448)], osend.at[t])
        for way in (0, 1):
            await_bytes(near.at[t, pl.ds(0, 7), 0], zsend.at[t, way])
            await_bytes(near.at[t, pl.ds(0, 7), 0], rsend.at[t, way])


def hand_over(a, b, c, a_out, b_out, c_out):
    a_out[...] = a[...]
    b_out[...] = b[...]
    c_out[...] = c[...]


def local(tokens, cotangent, expert_ids, combine, slot_table, swap_flags, weights, moments):
    vmem = pl.BlockSpec(memory_space=pltpu.VMEM)
    smem = pl.BlockSpec(memory_space=pltpu.SMEM)
    anyw = pl.BlockSpec(memory_space=pl.ANY)
    dma = pltpu.SemaphoreType.DMA
    layer_out, token_grad, update = pl.pallas_call(
        kernel,
        out_shape=(
            jax.ShapeDtypeStruct((TOK, D), bf16),
            jax.ShapeDtypeStruct((TOK, D), bf16),
            jax.ShapeDtypeStruct((PART, FF3), bf16),
        ),
        in_specs=[smem, smem, vmem, vmem, vmem, vmem, anyw, anyw],
        out_specs=(anyw, anyw, anyw),
        scratch_shapes=[
            pltpu.VMEM((16, 128), f32),
            pltpu.VMEM((NZ, 16, 128), f32),
            pltpu.VMEM((2, TOK, D), bf16),
            pltpu.VMEM((PART, FF3), bf16),
            pltpu.VMEM((2, 2, 128, HALF), bf16),
            pltpu.VMEM((NZ, 128, 128), bf16),
            pltpu.VMEM((2, 2, 128, HALF), bf16),
            pltpu.VMEM((NZ, 128, 128), bf16),
            pltpu.VMEM((NZ, 128, 128), bf16),
            pltpu.VMEM((NZ, 128, 128), bf16),
            pltpu.VMEM((NZ, 128, 128), f32),
            pltpu.VMEM((2, NZ, 2, TOK, HALF), bf16),
            pltpu.VMEM((2, 3, 128, D), bf16),
            pltpu.VMEM((2, ROWS, D), bf16),
            pltpu.VMEM((D, FF3), bf16),
            pltpu.VMEM((2, ROWS, D), bf16),
            pltpu.VMEM((2, 4, 128, D), bf16),
            pltpu.VMEM((2, 2, 4, 2, TOK, HALF), bf16),
            pltpu.VMEM((2, 2, 4, 2, TOK, HALF), bf16),
            pltpu.VMEM((3, PART, FF3), bf16),
            pltpu.VMEM((PART, FF3), f32),
            pltpu.VMEM((2, 6, PIECE, FF3), bf16),
            pltpu.VMEM((2, PART, FF3), f32),
            pltpu.VMEM((PART, FF3), bf16),
            pltpu.VMEM((PART, FF3), bf16),
            pltpu.VMEM((ROWS, FF2), f32),
            pltpu.VMEM((ROWS, FF), bf16),
            pltpu.VMEM((ROWS, FF2), bf16),
            dma((2,)),
            dma((2,)),
            dma((2, 2)),
            dma((2, 2, 4, 2)),
            dma((2,)),
            dma((2,)),
            dma((2,)),
            dma((2,)),
            dma((2, 2)),
            dma((2, 2)),
            dma((3,)),
            dma((2,)),
            dma((2, 3)),
            dma((2,)),
            dma((2, 4)),
            dma((2, 4)),
            dma((2, 2)),
            dma((2, 2, 4, 2)),
            dma((2,)),
            dma((2, 6)),
            dma((1,)),
            dma((4,)),
        ],
        compiler_params=pltpu.CompilerParams(
            collective_id=0, has_side_effects=True, vmem_limit_bytes=62 * 2**20
        ),
        cost_estimate=pl.CostEstimate(flops=8 * 10**9, bytes_accessed=9 * 10**6, transcendentals=10**6),
        name="moe_step",
    )(swap_flags, slot_table, expert_ids.T, combine.T, tokens, cotangent, weights[0], moments[:, 0])
    return pl.pallas_call(
        hand_over,
        out_shape=(
            jax.ShapeDtypeStruct((TOK, D), bf16),
            jax.ShapeDtypeStruct((TOK, D), bf16),
            jax.ShapeDtypeStruct((1, PART, FF3), bf16),
        ),
        in_specs=[vmem] * 3,
        out_specs=(vmem,) * 3,
        name="hand_over",
    )(layer_out, token_grad, update[None])


def solution(mesh):
    in_specs = (
        P(("dp", "expert"), None),
        P(("dp", "expert"), None),
        P(("dp", "expert"), None),
        P(("dp", "expert"), None),
        P(),
        P(),
        P("expert", "dp", None),
        P(None, "expert", "dp", None),
    )
    out_specs = (P(("dp", "expert"), None), P(("dp", "expert"), None), P("expert", "dp", None))
    return jax.shard_map(local, mesh=mesh, in_specs=in_specs, out_specs=out_specs, check_vma=False)
```

```python
import functools

import jax
import jax.numpy as jnp
from jax import lax
from jax.experimental import pallas as pl
from jax.experimental.pallas import tpu as pltpu
from jax.sharding import PartitionSpec as P

beta_one = 0.9
beta_two = 0.999
adam_eps = 1e-08
MESH = pl.DeviceIdType.MESH
bf16 = jnp.bfloat16
f32 = jnp.float32

NY, NX, NZ, NC = 4, 4, 8, 2
TOK = 64
D = 2048
HALF = D // 2
ROWS = 512
FF = 384
FF2 = 2 * FF
FF3 = 3 * FF
PART = D // NY
PIECE = PART // 4


def dot(a, b, ca=1, cb=0):
    return lax.dot_general(a, b, (((ca,), (cb,)), ((), ())), preferred_element_type=f32)


def kernel(
    flags, table, ids_ref, comb_ref, tok_ref, cot_ref, w_ref, mom_ref,
    lo_ref, tg_ref, up_ref,
    info_ref, info_all, sums, upd, fold, pick, xs_alone, back_one, back_hi, back_lo, scale,
    near, xs, xr, wg, orow, orecv, rs_out, rs_in,
    gsend, gown, grecv, mom, uown, urecv, proj, hidden, d_pre,
    local_sem, info_sem, zsend, zrecv, xsend, xrecv, xlocal, xsend_alone, frecv, flocal, out_sem, wsend, wrecv,
    osend, orecv_sem, olocal, rsend, rrecv, gsend_sem, grecv_sem, usend, urecv_sem,
):
    y = lax.axis_index("dp")
    e = lax.axis_index("expert")
    x = lax.div(e, NZ * NC)
    z = lax.div(lax.rem(e, NZ * NC), NC)
    c = lax.rem(e, NC)
    me = x * NC + c

    def xdev(j):
        return (y, lax.div(j, NC) * (NZ * NC) + z * NC + lax.rem(j, NC))

    def zdev(k):
        return (y, x * (NZ * NC) + k * NC + c)

    def zat(off):
        return lax.rem(z + (off % NZ), NZ)

    def yat(off):
        return lax.rem(y + (off % NY), NY)

    znext = (zdev(zat(1)), zdev(zat(-1)))
    ynext = ((yat(1), e), (yat(-1), e))

    def rcopy(src, dst, ssem, rsem, dev):
        return pltpu.make_async_remote_copy(
            src_ref=src, dst_ref=dst, send_sem=ssem, recv_sem=rsem, device_id=dev, device_id_type=MESH
        )

    def await_bytes(ref, sem):
        pltpu.make_async_copy(ref, ref, sem).wait()

    mom_copy = pltpu.make_async_copy(mom_ref, mom, local_sem.at[0])
    mom_copy.start()
    w_copy = pltpu.make_async_copy(w_ref, wg.at[pl.ds(y * PART, PART)], local_sem.at[1])
    w_copy.start()

    bar = pltpu.get_barrier_semaphore()
    for r in range(1, 8):
        for dev in (xdev(lax.rem(me + r, 8)), zdev(zat(r))):
            pl.semaphore_signal(bar, inc=1, device_id=dev, device_id_type=MESH)
    for dev in ynext:
        pl.semaphore_signal(bar, inc=1, device_id=dev, device_id_type=MESH)

    ids = ids_ref[...]

    def look_up(n, slot):
        return jnp.where(ids == n, table[n], slot)

    slot_of = lax.fori_loop(0, NX * NZ * NC, look_up, jnp.zeros((8, TOK), jnp.int32), unroll=4)
    info_ref[...] = jnp.full((16, 128), -1.0, f32)
    info_ref[0:8, :TOK] = slot_of.astype(f32)
    info_ref[8:16, :TOK] = comb_ref[...]

    pl.semaphore_wait(bar, 16)

    def send_own(t, h):
        src = (tok_ref, cot_ref)[t]
        for way in (0, 1):
            rcopy(
                src.at[:, pl.ds(h * HALF, HALF)], near.at[t, z, h],
                zsend.at[t, way], zrecv.at[t, way, 0, h], znext[way],
            ).start()

    send_own(0, 0)
    for r in range(1, NZ):
        rcopy(info_ref, info_all.at[z], info_sem.at[0], info_sem.at[1], zdev(zat(r))).start()
    def send_weights(first):
        for way in (0, 1):
            h = way if first else 1 - way
            rows = pl.ds(h * (PART // 2), PART // 2)
            rcopy(
                w_ref.at[rows], wg.at[pl.ds(y * PART + h * (PART // 2), PART // 2)],
                wsend.at[way], wrecv.at[way, h], ynext[way],
            ).start()

    send_weights(True)

    def weights_on():
        for way in (0, 1):
            base = yat(-1 if way == 0 else 1) * PART + way * (PART // 2)
            rows = wg.at[pl.ds(base, PART // 2)]
            await_bytes(rows, wrecv.at[way, way])
            rcopy(rows, rows, wsend.at[way], wrecv.at[way, 2], ynext[way]).start()

    def weights_in():
        w_copy.wait()
        for way in (0, 1):
            base = yat(-1 if way == 0 else 1) * PART + (1 - way) * (PART // 2)
            await_bytes(wg.at[pl.ds(base, PART // 2)], wrecv.at[way, 1 - way])
            base = yat(2) * PART + way * (PART // 2)
            await_bytes(wg.at[pl.ds(base, PART // 2)], wrecv.at[way, 2])

    info_all[z] = info_ref[...]
    before = (
        lax.broadcasted_iota(jnp.int32, (128, 128), 0) < lax.broadcasted_iota(jnp.int32, (128, 128), 1)
    ).astype(f32)
    j_col = lax.broadcasted_iota(jnp.int32, (8, 128), 0)
    slots = ((j_col // NC) * (NZ * NC) + z * NC + j_col % NC).astype(f32)
    place = lax.broadcasted_iota(jnp.int32, (16, 128), 0)

    def tables(off, carry):
        off = jnp.asarray(off, jnp.int32)
        one = info_all[lax.rem(z + off, NZ)]
        here = jnp.zeros((8, 128), f32)
        weight = jnp.zeros((8, 128), f32)
        for k in range(8):
            same = jnp.broadcast_to(one[k : k + 1], (8, 128)) == slots
            here = here + jnp.where(same, 1.0, 0.0)
            weight = weight + jnp.where(same, jnp.broadcast_to(one[8 + k : 9 + k], (8, 128)), 0.0)
        rank = dot(here, before)
        second = jnp.where((off >= 1) & (off <= 4), 1, 0)
        rank = jnp.where(here > 0.5, rank, 99.0)
        wanted = (place - second * 8).astype(f32)
        wanted = jnp.where((wanted >= 0.0) & (wanted < 8.0), wanted, -1.0)
        hot = []
        heavy = []
        for j in range(8):
            is_it = jnp.broadcast_to(rank[j : j + 1], (16, 128)) == wanted
            hot.append(jnp.where(is_it, 1.0, 0.0))
            heavy.append(jnp.where(is_it, jnp.broadcast_to(weight[j : j + 1], (16, 128)), 0.0))
        hot = jnp.concatenate(hot, axis=0)
        heavy = jnp.concatenate(heavy, axis=0)
        pick[off] = hot.astype(bf16)
        scale[off] = jnp.broadcast_to(jnp.sum(heavy, axis=1, keepdims=True), (128, 128))
        back_one[off] = hot.T.astype(bf16)
        turned = heavy.T
        high = turned.astype(bf16)
        back_hi[off] = high
        back_lo[off] = (turned - high.astype(f32)).astype(bf16)
        return carry

    tables(0, 0)
    def pack(t, off_a, rows_a, off_b, rows_b):
        rows = dot(pick[off_a][:, :TOK], rows_a) + dot(pick[off_b][:, :TOK], rows_b)
        if t == 1:
            weight = scale[off_a][:, :1]
            rows = rows * (weight if off_a == off_b else weight + scale[off_b][:, :1])
        return rows.astype(bf16)

    def spread(src, dst, there, sems):
        ssem, rsem, lsem = sems

        def send(r, carry):
            j = lax.rem(me + r, 8)
            rcopy(src(j), dst(there), ssem, rsem, xdev(j)).start()
            return carry

        lax.fori_loop(1, 8, send, 0)
        pltpu.make_async_copy(src(me), dst(there), lsem).start()

    def gather(t, s, h, off_a, off_b, rows_a, rows_b):
        cols = pl.ds(h * HALF, HALF)
        xs[t, s - 1, :, cols] = pack(t, off_a, rows_a, off_b, rows_b)
        spread(
            lambda j: xs.at[t, s - 1, pl.ds(j * 16, 16), cols], lambda at: xr.at[t, pl.ds(at, 16), cols],
            me * 64 + s * 16, (xsend.at[t], xrecv.at[t], xlocal.at[t]),
        )

    def gather_alone(t, which, off, low, high):
        cut = 120 if which == 0 else 8

        def turn(value):
            return jnp.concatenate([value[cut:], value[:cut]], axis=0)

        rows = dot(pick[off][:, :TOK], low) + dot(turn(pick[off])[:, :TOK], high)
        if t == 1:
            weight = scale[off]
            rows = rows * (weight + turn(weight))[:, :1]
        xs_alone[t, which] = rows.astype(bf16)
        spread(
            lambda j: xs_alone.at[t, which, pl.ds(j * 16, 16)], lambda at: fold.at[t, which, pl.ds(at, 16)],
            me * 16, (xsend_alone.at[t], frecv.at[t, which], flocal.at[t, which]),
        )

    def pass_chunks(t, s, h):
        for way in (0, 1):
            chunk = near.at[t, zat(-s if way == 0 else s), h]
            await_bytes(chunk, zrecv.at[t, way, s - 1, h])
            if s < 3 or h == way:
                rcopy(chunk, chunk, zsend.at[t, way], zrecv.at[t, way, s, h], znext[way]).start()

    def collect(t, s, h):
        gather(t, s, h, NZ - s, s, near[t, zat(-s), h], near[t, zat(s), h])

    def own_step(t):
        src = (tok_ref, cot_ref)[t]
        gather_alone(t, 0, 0, src[:, :HALF], src[:, HALF:])

    def far_step(t):
        far = zat(4)
        for h in (0, 1):
            await_bytes(near.at[t, far, h], zrecv.at[t, h, 3, h])
        gather_alone(t, 1, 4, near[t, far, 0], near[t, far, 1])

    def rows_in(t):
        for which in (0, 1):
            await_bytes(fold.at[t, which, pl.ds(0, 112)], frecv.at[t, which])
            await_bytes(fold.at[t, which, pl.ds(0, 16)], flocal.at[t, which])

        def unfold(j, carry):
            block = pl.ds(pl.multiple_of(j * 16, 16), 16)
            own, far = fold[t, 0, block].astype(f32), fold[t, 1, block].astype(f32)
            into = pl.ds(pl.multiple_of(j * 64, 64), 16)
            xr[t, into, :HALF] = jnp.concatenate([own[:8], far[8:]], axis=0).astype(bf16)
            xr[t, into, HALF:] = jnp.concatenate([own[8:], far[:8]], axis=0).astype(bf16)
            return carry

        lax.fori_loop(0, 8, unfold, 0)
        await_bytes(xr.at[t, pl.ds(0, 336)], xrecv.at[t])
        await_bytes(xr.at[t, pl.ds(0, 48)], xlocal.at[t])

    def forward():
        rows_in(0)
        weights_in()

        def project(n, carry):
            cols = pl.ds(pl.multiple_of(n * 256, 256), 256)
            proj[:, cols] = dot(xr[0], wg[:, cols])
            return carry

        lax.fori_loop(0, 3, project, 0)

        def activate(n, carry):
            rows = pl.ds(pl.multiple_of(n * 64, 64), 64)
            gate = proj[rows, :FF]
            hidden[rows] = (gate * jax.nn.sigmoid(gate) * proj[rows, FF:]).astype(bf16)
            return carry

        lax.fori_loop(0, 8, activate, 0)

        def out_rows(n, carry):
            part = pl.ds(pl.multiple_of(n * 256, 256), 256)
            orow[0, :, part] = dot(hidden[...], wg[part, FF2:], 1, 1).astype(bf16)
            return carry

        lax.fori_loop(0, 8, out_rows, 0)

    def send_back(t, s):
        spread(
            lambda j: orow.at[t, pl.ds(j * 64 + s * 16, 16)], lambda at: orecv.at[t, s, pl.ds(at, 16)],
            me * 16, (osend.at[t], orecv_sem.at[t, s], olocal.at[t, s]),
        )

    send_own(0, 1)
    own_step(0)
    own_step(1)
    await_bytes(info_all.at[pl.ds(0, NZ - 1)], info_sem.at[1])
    lax.fori_loop(1, NZ, tables, 0)
    pass_chunks(0, 1, 0)
    collect(0, 1, 0)
    pass_chunks(0, 1, 1)
    collect(0, 1, 1)
    send_weights(False)
    send_own(1, 0)
    send_own(1, 1)
    pass_chunks(0, 2, 0)
    collect(0, 2, 0)
    pass_chunks(0, 2, 1)
    collect(0, 2, 1)
    weights_on()
    pass_chunks(1, 1, 0)
    collect(1, 1, 0)
    pass_chunks(1, 1, 1)
    collect(1, 1, 1)
    pass_chunks(0, 3, 0)
    collect(0, 3, 0)
    pass_chunks(0, 3, 1)
    collect(0, 3, 1)
    pass_chunks(1, 2, 0)
    collect(1, 2, 0)
    pass_chunks(1, 2, 1)
    collect(1, 2, 1)
    far_step(0)
    pass_chunks(1, 3, 0)
    collect(1, 3, 0)
    pass_chunks(1, 3, 1)
    collect(1, 3, 1)
    far_step(1)
    forward()
    send_back(0, 0)
    send_back(0, 3)

    rows_in(1)

    def backward(n, carry):
        rows = pl.ds(pl.multiple_of(n * 256, 256), 256)
        d_hidden = dot(xr[1, rows], wg[:, FF2:])
        gate = proj[rows, :FF]
        up = proj[rows, FF:]
        sig = jax.nn.sigmoid(gate)
        d_pre[rows, :FF] = (d_hidden * up * (sig * (1.0 + gate * (1.0 - sig)))).astype(bf16)
        d_pre[rows, FF:] = (d_hidden * (gate * sig)).astype(bf16)
        return carry

    lax.fori_loop(0, 2, backward, 0)

    def weight_grad(off, dest):
        base = yat(off) * PART

        def half(n, carry):
            cols = pl.ds(pl.multiple_of(base + n * 256, 256), 256)
            rows = pl.ds(pl.multiple_of(n * 256, 256), 256)
            dest[rows, :FF2] = dot(xr[0, :, cols], d_pre[...], 0, 0).astype(dest.dtype)
            dest[rows, FF2:] = dot(xr[1, :, cols], hidden[...], 0, 0).astype(dest.dtype)
            return carry

        lax.fori_loop(0, 2, half, 0)

    def send_grad(way, message, block, piece):
        rcopy(
            gsend.at[block, pl.ds(piece * PIECE, PIECE)], grecv.at[way, message],
            gsend_sem.at[way], grecv_sem.at[way, message], ynext[way],
        ).start()

    def pass_on(first):
        for way in (0, 1):
            message = 0 if first else 3
            piece = (0 if way == 0 else 2) + (0 if first else 1)
            await_bytes(grecv.at[way, message], grecv_sem.at[way, message])

            def add(n, carry, way=way, message=message, piece=piece):
                there = pl.ds(pl.multiple_of(piece * PIECE + n * 16, 16), 16)
                here = pl.ds(pl.multiple_of(n * 16, 16), 16)
                total = gsend[1 + way, there].astype(f32) + grecv[way, message, here].astype(f32)
                gsend[1 + way, there] = total.astype(bf16)
                return carry

            lax.fori_loop(0, PIECE // 16, add, 0)
            send_grad(way, message + 2, 1 + way, piece)

    def second_round():
        send_grad(0, 3, 0, 1)
        send_grad(1, 3, 0, 3)
        send_grad(0, 4, 1, 3)
        send_grad(1, 4, 2, 1)

    def adam(first):
        for low in (True, False):
            piece = (0 if low else 2) + (0 if first else 1)
            done, plain = (2, 1) if first else (5, 4)
            from_low, from_high = (done, plain) if low else (plain, done)
            await_bytes(grecv.at[0, from_low], grecv_sem.at[0, from_low])
            await_bytes(grecv.at[1, from_high], grecv_sem.at[1, from_high])

            def rows_of(n, carry, piece=piece, from_low=from_low, from_high=from_high):
                there = pl.ds(pl.multiple_of(piece * PIECE + n * 16, 16), 16)
                here = pl.ds(pl.multiple_of(n * 16, 16), 16)
                grad = gown[there] + grecv[0, from_low, here].astype(f32) + grecv[1, from_high, here].astype(f32)
                first_new = beta_one * mom[0, there] + (1.0 - beta_one) * grad
                second_new = beta_two * mom[1, there] + (1.0 - beta_two) * grad * grad
                uown[there] = (first_new / (jnp.sqrt(second_new) + adam_eps)).astype(bf16)
                return carry

            lax.fori_loop(0, PIECE // 16, rows_of, 0)
            rows = pl.ds(piece * PIECE, PIECE)
            rcopy(
                uown.at[rows], urecv.at[rows], usend.at[0], urecv_sem.at[piece],
                xdev(lax.rem(me + 4, 8)),
            ).start()

    def partial(t, off, s, cols):
        rows = orecv[t, s, :, cols]
        if t == 1:
            return dot(back_one[off][:TOK], rows)
        return dot(back_hi[off][:TOK], rows) + dot(back_lo[off][:TOK], rows)

    def over_tiles(h, body):
        def tile(n, carry):
            inner = pl.multiple_of(n * 256, 256)
            body(pl.ds(pl.multiple_of(h * HALF + inner, 256), 256), pl.ds(inner, 256))
            return carry

        lax.fori_loop(0, HALF // 256, tile, 0)

    def reduce_step(t, k):
        s = (4 - k) % 4
        await_bytes(orecv.at[t, s, pl.ds(0, 112)], orecv_sem.at[t, s])
        await_bytes(orecv.at[t, s, pl.ds(0, 16)], olocal.at[t, s])
        for turn in (0, 1):
            for way in (0, 1):
                off = (4 - k) if way == 0 else (4 + k)
                h = way if turn == 1 else 1 - way
                if k == 0 and h != way:
                    continue
                adds = k > 1 or (k == 1 and h == way)
                if adds:
                    await_bytes(rs_in.at[t, way, k - 1, h], rrecv.at[t, way, k - 1, h])

                def one(cols, inner):
                    total = partial(t, off, s, cols)
                    if adds:
                        total = total + rs_in[t, way, k - 1, h, :, inner].astype(f32)
                    rs_out[t, way, k, h, :, inner] = total.astype(bf16)

                over_tiles(h, one)
                rcopy(
                    rs_out.at[t, way, k, h], rs_in.at[t, way, k, h],
                    rsend.at[t, way], rrecv.at[t, way, k, h], znext[way],
                ).start()

    def reduce_last(t):
        for h in (0, 1):
            for way in (0, 1):
                await_bytes(rs_in.at[t, way, 3, h], rrecv.at[t, way, 3, h])

            def one(cols, inner):
                total = partial(t, 0, 0, cols)
                total = total + rs_in[t, 0, 3, h, :, inner].astype(f32) + rs_in[t, 1, 3, h, :, inner].astype(f32)
                sums[t, :, cols] = total.astype(bf16)

            over_tiles(h, one)
        pltpu.make_async_copy(sums.at[t], (lo_ref, tg_ref)[t], out_sem.at[t]).start()

    def dx_rows(n, carry):
        part = pl.ds(pl.multiple_of(n * 256, 256), 256)
        orow[1, :, part] = dot(d_pre[...], wg[part, :FF2], 1, 1).astype(bf16)
        return carry

    weight_grad(2, gsend.at[0])
    send_grad(0, 0, 0, 0)
    send_grad(1, 0, 0, 2)
    send_back(0, 2)
    lax.fori_loop(0, 8, dx_rows, 0)
    weight_grad(1, gsend.at[1])
    weight_grad(-1, gsend.at[2])
    send_grad(0, 1, 1, 2)
    send_grad(1, 1, 2, 0)
    send_back(0, 1)
    reduce_step(0, 0)
    send_back(1, 0)
    pass_on(True)
    reduce_step(0, 1)
    send_back(1, 3)
    weight_grad(0, gown)
    mom_copy.wait()
    reduce_step(0, 2)
    second_round()
    send_back(1, 2)
    reduce_step(0, 3)
    send_back(1, 1)
    adam(True)
    pass_on(False)
    reduce_step(1, 0)
    reduce_last(0)
    reduce_step(1, 1)
    reduce_step(1, 2)
    adam(False)
    reduce_step(1, 3)
    reduce_last(1)

    swapped = jnp.full((16, FF3), flags[lax.rem(e, NX * NZ * NC // 2)], jnp.int32) == 1
    for piece in (0, 2, 1, 3):
        await_bytes(urecv.at[pl.ds(piece * PIECE, PIECE)], urecv_sem.at[piece])

        def choose(n, carry, piece=piece):
            there = pl.ds(pl.multiple_of(piece * PIECE + n * 16, 16), 16)
            upd[there] = jnp.where(swapped, urecv[there].astype(f32), uown[there].astype(f32)).astype(bf16)
            return carry

        lax.fori_loop(0, PIECE // 16, choose, 0)
        rows = pl.ds(piece * PIECE, PIECE)
        pltpu.make_async_copy(upd.at[rows], up_ref.at[rows], out_sem.at[2]).start()

    for t in (0, 1):
        await_bytes(sums.at[t], out_sem.at[t])
    await_bytes(upd, out_sem.at[2])
    await_bytes(info_all.at[pl.ds(0, NZ - 1)], info_sem.at[0])
    await_bytes(uown, usend.at[0])
    for way in (0, 1):
        await_bytes(wg.at[pl.ds(0, PART + PART // 2)], wsend.at[way])
        await_bytes(grecv.at[way], gsend_sem.at[way])
    for t in (0, 1):
        await_bytes(xr.at[t, pl.ds(0, 336)], xsend.at[t])
        await_bytes(xs_alone.at[t, :, pl.ds(0, 112)], xsend_alone.at[t])
        await_bytes(orow.at[t, pl.ds(0, 448)], osend.at[t])
        for way in (0, 1):
            await_bytes(near.at[t, pl.ds(0, 7), 0], zsend.at[t, way])
            await_bytes(near.at[t, pl.ds(0, 7), 0], rsend.at[t, way])


def hand_over(a, b, c, a_out, b_out, c_out, a_mid, b_mid, c_mid, in_sem, out_sem):
    parts = [(c.at[0, pl.ds(n * PIECE, PIECE)], c_mid.at[pl.ds(n * PIECE, PIECE)], c_out.at[0, pl.ds(n * PIECE, PIECE)])
             for n in range(4)] + [(a, a_mid, a_out), (b, b_mid, b_out)]
    first = [pltpu.make_async_copy(src, mid, in_sem.at[n]) for n, (src, mid, _) in enumerate(parts)]
    second = [pltpu.make_async_copy(mid, dst, out_sem.at[n]) for n, (_, mid, dst) in enumerate(parts)]
    for copy in first:
        copy.start()
    for n, copy in enumerate(first):
        copy.wait()
        second[n].start()
    for copy in second:
        copy.wait()


def local(tokens, cotangent, expert_ids, combine, slot_table, swap_flags, weights, moments):
    vmem = pl.BlockSpec(memory_space=pltpu.VMEM)
    smem = pl.BlockSpec(memory_space=pltpu.SMEM)
    anyw = pl.BlockSpec(memory_space=pl.ANY)
    dma = pltpu.SemaphoreType.DMA
    layer_out, token_grad, update = pl.pallas_call(
        kernel,
        out_shape=(
            jax.ShapeDtypeStruct((TOK, D), bf16),
            jax.ShapeDtypeStruct((TOK, D), bf16),
            jax.ShapeDtypeStruct((PART, FF3), bf16),
        ),
        in_specs=[smem, smem, vmem, vmem, vmem, vmem, anyw, anyw],
        out_specs=(anyw, anyw, anyw),
        scratch_shapes=[
            pltpu.VMEM((16, 128), f32),
            pltpu.VMEM((NZ, 16, 128), f32),
            pltpu.VMEM((2, TOK, D), bf16),
            pltpu.VMEM((PART, FF3), bf16),
            pltpu.VMEM((2, 2, 128, HALF), bf16),
            pltpu.VMEM((NZ, 128, 128), bf16),
            pltpu.VMEM((2, 2, 128, HALF), bf16),
            pltpu.VMEM((NZ, 128, 128), bf16),
            pltpu.VMEM((NZ, 128, 128), bf16),
            pltpu.VMEM((NZ, 128, 128), bf16),
            pltpu.VMEM((NZ, 128, 128), f32),
            pltpu.VMEM((2, NZ, 2, TOK, HALF), bf16),
            pltpu.VMEM((2, 3, 128, D), bf16),
            pltpu.VMEM((2, ROWS, D), bf16),
            pltpu.VMEM((D, FF3), bf16),
            pltpu.VMEM((2, ROWS, D), bf16),
            pltpu.VMEM((2, 4, 128, D), bf16),
            pltpu.VMEM((2, 2, 4, 2, TOK, HALF), bf16),
            pltpu.VMEM((2, 2, 4, 2, TOK, HALF), bf16),
            pltpu.VMEM((3, PART, FF3), bf16),
            pltpu.VMEM((PART, FF3), f32),
            pltpu.VMEM((2, 6, PIECE, FF3), bf16),
            pltpu.VMEM((2, PART, FF3), f32),
            pltpu.VMEM((PART, FF3), bf16),
            pltpu.VMEM((PART, FF3), bf16),
            pltpu.VMEM((ROWS, FF2), f32),
            pltpu.VMEM((ROWS, FF), bf16),
            pltpu.VMEM((ROWS, FF2), bf16),
            dma((2,)),
            dma((2,)),
            dma((2, 2)),
            dma((2, 2, 4, 2)),
            dma((2,)),
            dma((2,)),
            dma((2,)),
            dma((2,)),
            dma((2, 2)),
            dma((2, 2)),
            dma((3,)),
            dma((2,)),
            dma((2, 3)),
            dma((2,)),
            dma((2, 4)),
            dma((2, 4)),
            dma((2, 2)),
            dma((2, 2, 4, 2)),
            dma((2,)),
            dma((2, 6)),
            dma((1,)),
            dma((4,)),
        ],
        compiler_params=pltpu.CompilerParams(
            collective_id=0, has_side_effects=True, vmem_limit_bytes=62 * 2**20
        ),
        cost_estimate=pl.CostEstimate(flops=8 * 10**9, bytes_accessed=9 * 10**6, transcendentals=10**6),
        name="moe_step",
    )(swap_flags, slot_table, expert_ids.T, combine.T, tokens, cotangent, weights[0], moments[:, 0])
    return pl.pallas_call(
        hand_over,
        out_shape=(
            jax.ShapeDtypeStruct((TOK, D), bf16),
            jax.ShapeDtypeStruct((TOK, D), bf16),
            jax.ShapeDtypeStruct((1, PART, FF3), bf16),
        ),
        in_specs=[anyw] * 3,
        out_specs=(anyw,) * 3,
        scratch_shapes=[
            pltpu.VMEM((TOK, D), bf16),
            pltpu.VMEM((TOK, D), bf16),
            pltpu.VMEM((PART, FF3), bf16),
            dma((6,)),
            dma((6,)),
        ],
        name="hand_over",
    )(layer_out, token_grad, update[None])


def solution(mesh):
    in_specs = (
        P(("dp", "expert"), None),
        P(("dp", "expert"), None),
        P(("dp", "expert"), None),
        P(("dp", "expert"), None),
        P(),
        P(),
        P("expert", "dp", None),
        P(None, "expert", "dp", None),
    )
    out_specs = (P(("dp", "expert"), None), P(("dp", "expert"), None), P("expert", "dp", None))
    return jax.shard_map(local, mesh=mesh, in_specs=in_specs, out_specs=out_specs, check_vma=False)
```
